256 devices in a mesh: ctx: 32 (over x, y, z_hi), exp: 8 (over z_lo, core).
Axes of the slice: x: 4, y: 4, z: 8 (z_hi: 2, z_lo: 4; z = z_hi * 4 + z_lo), core: 2. Of those that a mesh axis runs over, the one named last changes fastest.
Arguments:
- queries: bfloat16 [2048, 5120], P('ctx', 'exp')
- keys: bfloat16 [2048, 1024], P('ctx', 'exp')
- values: bfloat16 [2048, 1024], P('ctx', 'exp'), may hold values from -6 to 6
- residual: bfloat16 [2048, 5120], P(('ctx', 'exp')), may hold values from -4 to 4
- span_order: int32 [32, 2], replicated, may hold values from 0 to 63, as said below
- out_weight: bfloat16 [5120, 5120], P('exp', 'ctx'), may hold values from -0.078125 to 0.078125
- norm_gain: bfloat16 [5120], replicated, may hold values from 0.099609375 to 1.8984375
- router: bfloat16 [5120, 8], replicated, may hold values from -0.078125 to 0.078125
- expert_ids: int32 [2048, 1], P(('ctx', 'exp')), may hold values from 0 to 7; in each aligned block of 8 rows (0 to 7, 8 to 15, ...) at most 2 rows name the same one
- expert_gate: bfloat16 [8, 5120, 8192], P('exp', None, 'ctx'), may hold values from -0.078125 to 0.078125
- expert_up: bfloat16 [8, 5120, 8192], P('exp', None, 'ctx'), may hold values from -0.078125 to 0.078125
- expert_down: bfloat16 [8, 8192, 5120], P('exp', 'ctx'), may hold values from -0.0625 to 0.0625
- shared_gate: bfloat16 [5120, 4096], P(None, 'ctx'), may hold values from -0.078125 to 0.078125
- shared_up: bfloat16 [5120, 4096], P(None, 'ctx'), may hold values from -0.078125 to 0.078125
- shared_down: bfloat16 [4096, 5120], P('ctx'), may hold values from -0.09375 to 0.09375
Outputs:
- layer_out: bfloat16 [2048, 5120], P(('ctx', 'exp'))
The draws below stay inside these ranges and needn't reach their ends.
Inputs may be any that keep to these rules, and one draw needn't show every extreme that they name: `span_order`: each row holds a block p and the block 63 - p, and every p of 0 to 31 appears in exactly one row. `expert_ids`: among the 8 rows of one device no expert is named by more than 2 rows, a bound that some block reaches.
All inputs are finite; a program needn't handle non-finite values.
Results may differ from the reference program's by a relative error of at most 0.035.
Values may be sent and summed in bfloat16 or wider, within the bound.
No kernel may reach another device: no remote copies, remote signals or barrier semaphores. Data moves between devices by JAX's collectives and lax.ppermute only.
A program may use at most 128 MiB of HBM per device.

```python
import math
import jax
import jax.numpy as jnp
import numpy as np
from jax import lax

D = 5120
H = 40
KVH = 8
HD = 128
FF = 8192
FS = 4096
EXPERTS = 8
TOK_DEV = 8
CAP = 2
SEQ = 2048
HALF = 32
N_CTX = 32
N_EXP = 8


def key_base(key):
    return 1.4 * jax.random.truncated_normal(key, -6.0, 6.0, (SEQ, KVH * HD), jnp.float32)


def draw_keys(key, part):
    return key_base(key).astype(jnp.bfloat16)


def draw_queries(key, part):
    key = jax.random.fold_in(key, 11)
    fresh = 1.4 * jax.random.truncated_normal(key, -6.0, 6.0, (SEQ, H * HD), jnp.float32)
    return fresh.astype(jnp.bfloat16)


def draw_span_order(key, part):
    key = jax.random.fold_in(key, 5)
    first = jax.random.permutation(key, N_CTX).astype(jnp.int32)
    return jnp.stack([first, 2 * N_CTX - 1 - first], axis=1).astype(jnp.int32)


def levels(key, dims, cuts, least, largest):
    gain, own = 1.0, jax.random.fold_in(key, 6)
    for dim, parts in cuts:
        heights = jnp.exp(jax.random.uniform(jax.random.fold_in(own, dim), (parts,), jnp.float32, least / len(cuts), largest / len(cuts)))
        gain = gain * jnp.repeat(heights, dims[dim] // parts).reshape([-1 if axis == dim else 1 for axis in range(len(dims))])
    return gain


def assign_block(key, own, number, rows, amount, top, most, skew):
    ranking = jax.random.permutation(key, amount)
    crowded, usual = shares(amount, rows * top, most, skew, True), shares(amount, rows * top, most, skew, False)
    places = jnp.arange(amount)

    def named(sizes, offset_by):
        used = int((sizes > 0).sum())
        fixed = max(1, used // 4)
        shifted = fixed + (places - fixed + offset_by * (used - fixed)) % max(1, amount - fixed)
        return jnp.zeros((amount,), jnp.int32).at[ranking[jnp.where(places < fixed, places, shifted)]].set(jnp.asarray(sizes, jnp.int32))

    sizes = jnp.where(number % 4 == 0, named(crowded, number // 4), named(usual, number - number // 4 - 1))
    mixed = jax.random.permutation(jax.random.fold_in(own, 3), amount)
    source_of, receiver = mixed[0:amount // 2 * 2:2], mixed[1:amount // 2 * 2:2]
    margin = jnp.minimum(sizes[source_of] - 1, most - sizes[receiver]) // 2
    margin = jnp.where((source_of == ranking[0]) | (receiver == ranking[0]) | (sizes[receiver] == 0), 0, jnp.maximum(margin, 0))
    shifted = jax.random.randint(jax.random.fold_in(own, 4), (amount // 2,), 0, 1 << 20) % (margin + 1)
    sizes = sizes.at[source_of].add(-shifted).at[receiver].add(shifted)
    items = jnp.searchsorted(jnp.cumsum(sizes), jnp.arange(rows * top), side="right").astype(jnp.int32)
    table = items.reshape(top, rows).T
    table = table[jax.random.permutation(jax.random.fold_in(own, 1), rows)]
    offset_by = jax.random.randint(jax.random.fold_in(own, 2), (rows, 1), 0, top)
    return jnp.take_along_axis(table, (jnp.arange(top)[None, :] + offset_by) % top, axis=1)


def shares(count, total, most, lean, full):
    portions = [(1 << 20) // math.isqrt(standing ** lean) + 1 for standing in range(1, count + 1)]
    largest = most if full else min(most, max(-(-total // count), total * portions[0] // sum(portions)))
    least = 1 if total - largest >= count - 1 else 0
    counts, spare = [largest] + [least] * (count - 1), total - largest - least * (count - 1)
    while spare > 0:
        free = [i for i in range(1, count) if counts[i] < largest] or [i for i in range(1, count) if counts[i] < most]
        mass, remaining = sum([portions[i] for i in free]), spare
        for i in free:
            extra = min(most - counts[i], max(1, remaining * portions[i] // mass), spare)
            counts[i] = counts[i] + extra
            spare = spare - extra
    return np.array(counts)


def normal_values(stream_key, extent, scale, bound, pieces=(), held_as=jnp.bfloat16):
    result = jax.random.normal(stream_key, extent, jnp.float32) * scale
    if len(pieces) > 0:
        result = levels(stream_key, extent, pieces, -0.22, 0.18) * result
    return jnp.clip(result, min=-bound, max=bound).astype(held_as)


def setup_inputs(seed: int = 0) -> dict:
    arg_keys = jax.random.split(jax.random.key(seed), 16)
    queries = draw_queries(jax.random.fold_in(arg_keys[15], 71), 0)
    keys = draw_keys(jax.random.fold_in(arg_keys[15], 71), 0)
    values = normal_values(arg_keys[2], (SEQ, KVH * HD), 1.0, 6.0, ((0, 32), (1, 8)))
    residual = normal_values(arg_keys[3], (SEQ, D), 0.3, 4.0, ((0, 256),))
    span_order = draw_span_order(jax.random.fold_in(arg_keys[15], 71), 0)
    out_weight = normal_values(arg_keys[5], (H * HD, D), (H * HD) ** -0.5, 0.078125, ((0, 8), (1, 32)))
    norm_gain = jnp.clip(1.0 + 0.18 * jax.random.normal(arg_keys[6], (D,), jnp.float32), 0.099609375, 1.8984375).astype(jnp.bfloat16)
    router = normal_values(arg_keys[7], (D, EXPERTS), D ** -0.5, 0.078125)
    expert_ids_keys = jax.random.split(jax.random.fold_in(arg_keys[8], 1), SEQ // TOK_DEV)
    expert_ids_turns = jax.random.permutation(jax.random.fold_in(arg_keys[8], 3), SEQ // TOK_DEV)
    expert_ids = jax.vmap(lambda own, number: assign_block(jax.random.fold_in(arg_keys[8], 2), own, number, TOK_DEV, EXPERTS, 1, CAP, 2))(expert_ids_keys, expert_ids_turns).reshape((SEQ, 1))
    expert_gate = normal_values(arg_keys[9], (EXPERTS, D, FF), D ** -0.5, 0.078125, ((0, 8), (2, 32)))
    expert_up = normal_values(arg_keys[10], (EXPERTS, D, FF), D ** -0.5, 0.078125, ((0, 8), (2, 32)))
    expert_down = normal_values(arg_keys[11], (EXPERTS, FF, D), FF ** -0.5, 0.0625, ((0, 8), (1, 32)))
    shared_gate = normal_values(arg_keys[12], (D, FS), D ** -0.5, 0.078125, ((1, 32),))
    shared_up = normal_values(arg_keys[13], (D, FS), D ** -0.5, 0.078125, ((1, 32),))
    shared_down = normal_values(arg_keys[14], (FS, D), FS ** -0.5, 0.09375, ((0, 32),))
    return dict(queries=queries, keys=keys, values=values, residual=residual, span_order=span_order, out_weight=out_weight, norm_gain=norm_gain, router=router, expert_ids=expert_ids, expert_gate=expert_gate, expert_up=expert_up, expert_down=expert_down, shared_gate=shared_gate, shared_up=shared_up, shared_down=shared_down)


def positions_of(span_order):
    flat = span_order.reshape(-1).astype(jnp.int32)
    return (flat[:, None] * HALF + jnp.arange(HALF, dtype=jnp.int32)[None, :]).reshape(-1)

def reference(queries, keys, values, residual, span_order, out_weight, norm_gain, router, expert_ids, expert_gate, expert_up, expert_down, shared_gate, shared_up, shared_down):
    position = positions_of(span_order)
    visible = position[None, :] <= position[:, None]
    group = H // KVH
    query_heads = queries.reshape(SEQ, H, HD)
    key_heads = keys.reshape(SEQ, KVH, HD)
    value_heads = values.reshape(SEQ, KVH, HD)
    scale = HD ** (-0.5)

    def one_head(head):
        kv_head = head // group
        query_one = lax.dynamic_index_in_dim(query_heads, head, 1, keepdims=False)
        key_one = lax.dynamic_index_in_dim(key_heads, kv_head, 1, keepdims=False)
        value_one = lax.dynamic_index_in_dim(value_heads, kv_head, 1, keepdims=False)
        scores = lax.dot_general(query_one, key_one, (((1,), (1,)), ((), ())), preferred_element_type=jnp.float32) * scale
        top = lax.optimization_barrier(jnp.max(jnp.where(visible, scores, -1e+30), axis=1, keepdims=True))
        weights = jnp.where(visible, jnp.exp(scores - top), 0.0)
        total = lax.optimization_barrier(jnp.sum(weights, axis=1, keepdims=True))
        mixed = jnp.dot(weights.astype(jnp.bfloat16), value_one, preferred_element_type=jnp.float32) / total
        return mixed.astype(jnp.bfloat16)
    attended = lax.map(one_head, jnp.arange(H, dtype=jnp.int32))
    attended = attended.transpose(1, 0, 2).reshape(SEQ, H * HD)
    projected = jnp.dot(attended, out_weight, preferred_element_type=jnp.float32)
    hidden = (residual.astype(jnp.float32) + projected).astype(jnp.bfloat16)
    wide = hidden.astype(jnp.float32)
    normed = (wide * lax.rsqrt(lax.optimization_barrier(jnp.mean(wide * wide, axis=1, keepdims=True)) + 1e-05) * norm_gain.astype(jnp.float32)).astype(jnp.bfloat16)
    logits = jnp.dot(normed, router, preferred_element_type=jnp.float32)
    chosen_ids = expert_ids[:, 0].astype(jnp.int32)
    picked = jnp.take_along_axis(logits, expert_ids.astype(jnp.int32), axis=1)[:, 0]
    score_gate = jax.nn.sigmoid(picked).astype(jnp.bfloat16)
    limit = N_CTX * N_EXP * CAP
    routed_block = FF // N_CTX
    shared_block = FS // N_CTX

    def one_expert(carry, expert):
        member = chosen_ids == expert
        rank = (jnp.cumsum(member.astype(jnp.int32)) - 1).astype(jnp.int32)
        target = jnp.where(member, rank, limit).astype(jnp.int32)
        slot_rows = jnp.zeros((limit + 1, D), jnp.bfloat16).at[target].set(normed)[:limit]
        slot_gate = jnp.zeros((limit + 1,), jnp.bfloat16).at[target].set(score_gate)[:limit]
        scaled = (slot_rows.astype(jnp.float32) * slot_gate.astype(jnp.float32)[:, None]).astype(jnp.bfloat16)
        gate_w = lax.dynamic_index_in_dim(expert_gate, expert, 0, keepdims=False)
        up_w = lax.dynamic_index_in_dim(expert_up, expert, 0, keepdims=False)
        down_w = lax.dynamic_index_in_dim(expert_down, expert, 0, keepdims=False)
        routed_hidden = (jax.nn.silu(jnp.dot(scaled, gate_w, preferred_element_type=jnp.float32)) * jnp.dot(scaled, up_w, preferred_element_type=jnp.float32)).astype(jnp.bfloat16)
        shared_hidden = (jax.nn.silu(jnp.dot(slot_rows, shared_gate, preferred_element_type=jnp.float32)) * jnp.dot(slot_rows, shared_up, preferred_element_type=jnp.float32)).astype(jnp.bfloat16)

        def add_block(total, block):
            routed_cols = lax.dynamic_slice_in_dim(routed_hidden, block * routed_block, routed_block, 1)
            routed_rows = lax.dynamic_slice_in_dim(down_w, block * routed_block, routed_block, 0)
            shared_cols = lax.dynamic_slice_in_dim(shared_hidden, block * shared_block, shared_block, 1)
            shared_rows = lax.dynamic_slice_in_dim(shared_down, block * shared_block, shared_block, 0)
            part = jnp.dot(routed_cols, routed_rows, preferred_element_type=jnp.float32) + jnp.dot(shared_cols, shared_rows, preferred_element_type=jnp.float32)
            rounded = lax.optimization_barrier(part.astype(jnp.bfloat16))
            return (total + rounded.astype(jnp.float32), None)
        slot_out, _ = lax.scan(add_block, jnp.zeros((limit, D), jnp.float32), jnp.arange(N_CTX, dtype=jnp.int32))
        back = slot_out[jnp.clip(rank, 0, limit - 1)]
        return (carry + jnp.where(member[:, None], back, 0.0), None)
    experts_out, _ = lax.scan(one_expert, jnp.zeros((SEQ, D), jnp.float32), jnp.arange(EXPERTS, dtype=jnp.int32))
    return (wide + experts_out).astype(jnp.bfloat16)
```

```python
import jax
import jax.numpy as jnp
from jax import lax
from jax.sharding import Mesh, PartitionSpec as P

H = 40
KVH = 8
HD = 128
F32 = jnp.float32
BF16 = jnp.bfloat16
AXES = ("x", "y", "zh", "zl", "core")
CTX = ("x", "y", "zh")
EXP = ("zl", "core")
LINE = ("zh", "zl", "core")


def shift(value, axis, by):
    n = lax.axis_size(axis)
    return lax.ppermute(value, axis, [(i, (i + by) % n) for i in range(n)])


def spread(value, axis):
    back = shift(value, axis, -1)
    ahead = shift(value, axis, 1)
    across = shift(value, axis, 2)
    return [value, ahead, across, back]


def collect(terms, axis):
    ahead = shift(terms[1], axis, -1)
    back = shift(terms[3], axis, 1)
    across = shift(terms[2], axis, 2)
    return (
        terms[0].astype(F32) + ahead.astype(F32) + back.astype(F32) + across.astype(F32)
    ).astype(BF16)


def placed(parts, axis, dim):
    me = lax.axis_index(axis)
    n = len(parts)
    shape = list(parts[0].shape)
    size = shape[dim]
    shape[dim] = size * n
    out = jnp.zeros(shape, parts[0].dtype)
    for k, part in enumerate(parts):
        out = lax.dynamic_update_slice_in_dim(out, part, lax.rem(me - k + n, n) * size, dim)
    return out


def in_order(mine, other, index):
    return jnp.where(index == 0, jnp.stack([mine, other]), jnp.stack([other, mine]))


def body(
    queries,
    keys,
    values,
    residual,
    span_order,
    out_weight,
    norm_gain,
    router,
    expert_ids,
    expert_gate,
    expert_up,
    expert_down,
    shared_gate,
    shared_up,
    shared_down,
):
    zh, core = lax.axis_index("zh"), lax.axis_index("core")
    rows = queries.shape[0]
    half = rows // 2
    group = H // KVH
    scale = HD ** (-0.5)
    features = residual.shape[1]

    pair = jnp.concatenate([keys, values], axis=1)
    pair_other = shift(pair, "zh", 1)
    both = jnp.concatenate([pair, pair_other], axis=0)
    sixteen = jnp.broadcast_to(both[None], (16,) + both.shape)
    everyone = lax.all_to_all(sixteen, ("x", "y"), split_axis=0, concat_axis=0)
    everyone = everyone.reshape(-1, 2 * HD)
    all_keys, all_values = everyone[:, :HD], everyone[:, HD:]
    spans = span_order.reshape(16, 2, 2)
    spans = jnp.where(zh == 0, spans, spans[:, ::-1])
    key_pos = (
        spans.reshape(-1)[:, None] * half + jnp.arange(half, dtype=jnp.int32)[None, :]
    ).reshape(-1)
    own = lax.dynamic_index_in_dim(span_order, lax.axis_index(CTX), 0, keepdims=False)
    own_pos = (own[:, None] * half + jnp.arange(half, dtype=jnp.int32)[None, :]).reshape(-1)

    turned = out_weight.T
    width = turned.shape[0] // 2
    w_mine = lax.dynamic_slice_in_dim(turned, core * width, width, 0)
    w_given = lax.dynamic_slice_in_dim(turned, (1 - core) * width, width, 0)
    w_other = shift(w_given, "core", 1)
    w_mine = placed(spread(w_mine[None, None], "x"), "x", 0)
    w_other = placed(spread(w_other[None, None], "y"), "y", 1)
    w_mine = placed(spread(w_mine, "y"), "y", 1).reshape(-1, turned.shape[1])
    w_other = placed(spread(w_other, "x"), "x", 0).reshape(-1, turned.shape[1])

    query_pos = jnp.tile(own_pos, group)
    grouped = queries.reshape(rows, group, HD).transpose(1, 0, 2).reshape(group * rows, HD)
    contract = (((1,), (1,)), ((), ()))
    visible = key_pos[None, :] <= query_pos[:, None]
    scores = lax.dot_general(grouped, all_keys, contract, preferred_element_type=F32) * scale
    top = jnp.max(jnp.where(visible, scores, -1e30), axis=1, keepdims=True)
    weights = jnp.where(visible, jnp.exp(scores - top), 0.0)
    total = jnp.sum(weights, axis=1, keepdims=True)
    mixed = jnp.dot(weights.astype(BF16), all_values, preferred_element_type=F32) / total
    attended = (
        mixed.astype(BF16).reshape(group, rows, HD).transpose(1, 0, 2).reshape(rows, group * HD)
    )

    far = shift(attended, "zh", 1)
    near = shift(attended, "core", 1)
    far_near = shift(far, "core", 1)
    a_mine = in_order(attended, far, zh).reshape(2 * rows, -1)
    a_other = in_order(near, far_near, zh).reshape(2 * rows, -1)
    partial = lax.dot_general(a_mine, w_mine, contract, preferred_element_type=F32)
    partial += lax.dot_general(a_other, w_other, contract, preferred_element_type=F32)
    partial = partial.astype(BF16).reshape(16, rows // 8, -1)
    pieces = lax.all_to_all(partial, LINE, split_axis=0, concat_axis=0)
    pieces = pieces.reshape(2, 4, 2, rows // 8, 16, width).astype(F32)
    projected = jnp.sum(pieces, axis=1).transpose(2, 3, 0, 1, 4).reshape(rows // 8, features)

    wide = (residual.astype(F32) + projected).astype(BF16).astype(F32)
    normed = (
        wide
        * lax.rsqrt(jnp.mean(wide * wide, axis=1, keepdims=True) + 1e-05)
        * norm_gain.astype(F32)
    ).astype(BF16)

    capacity = 2
    experts = router.shape[1]
    chosen = expert_ids[:, 0]
    onehot = (chosen[:, None] == jnp.arange(experts, dtype=jnp.int32)[None, :]).astype(jnp.int32)
    ranking = jnp.sum(jnp.cumsum(onehot, axis=0) * onehot, axis=1) - 1
    slot_index = chosen * capacity + ranking
    placing = slot_index[None, :] == jnp.arange(experts * capacity, dtype=jnp.int32)[:, None]
    send = jnp.dot(placing.astype(BF16), normed, preferred_element_type=F32).astype(BF16)
    send = send.reshape(1, experts, capacity, features)
    send = jnp.broadcast_to(send, (2, experts, capacity, features)).reshape(16, capacity, features)
    arrived = lax.all_to_all(send, LINE, split_axis=0, concat_axis=0)
    first, second = arrived[:, 0], arrived[:, 1]

    first = jnp.concatenate(spread(first, "x"), axis=0)
    second = jnp.concatenate(spread(second, "y"), axis=0)
    first = spread(first, "y")
    second = spread(second, "x")
    mine = lax.axis_index(EXP)
    router_mine = lax.dynamic_slice_in_dim(router, mine, 1, 1)

    def experts_of(slots):
        gate = jax.nn.sigmoid(jnp.dot(slots, router_mine, preferred_element_type=F32)).astype(BF16)
        scaled = (slots.astype(F32) * gate.astype(F32)).astype(BF16)
        hidden = (
            jax.nn.silu(jnp.dot(scaled, expert_gate[0], preferred_element_type=F32))
            * jnp.dot(scaled, expert_up[0], preferred_element_type=F32)
        ).astype(BF16)
        shared = (
            jax.nn.silu(jnp.dot(slots, shared_gate, preferred_element_type=F32))
            * jnp.dot(slots, shared_up, preferred_element_type=F32)
        ).astype(BF16)
        return (
            jnp.dot(hidden, expert_down[0], preferred_element_type=F32)
            + jnp.dot(shared, shared_down, preferred_element_type=F32)
        ).astype(BF16)

    outs = [experts_of(jnp.concatenate([a, b], axis=0)) for a, b in zip(first, second)]
    count = first[0].shape[0]
    first = collect([o[:count] for o in outs], "y")
    second = collect([o[count:] for o in outs], "x")
    quarter = count // 4
    first = collect([first[k * quarter : (k + 1) * quarter] for k in range(4)], "x")
    second = collect([second[k * quarter : (k + 1) * quarter] for k in range(4)], "y")
    back = lax.all_to_all(
        jnp.stack([first, second], axis=1), LINE, split_axis=0, concat_axis=0
    )
    back = jnp.sum(back.reshape(2, experts * capacity, features).astype(F32), axis=0)
    experts_out = jnp.dot(
        placing.astype(F32).T, back, precision=lax.Precision.HIGHEST, preferred_element_type=F32
    )
    return (wide + experts_out).astype(BF16)


def solution(mesh):
    fine = Mesh(mesh.devices.reshape(4, 4, 2, 4, 2), AXES)
    return jax.shard_map(
        body,
        mesh=fine,
        in_specs=(
            P(CTX, EXP),
            P(CTX, EXP),
            P(CTX, EXP),
            P(AXES, None),
            P(),
            P(EXP, CTX),
            P(),
            P(),
            P(AXES, None),
            P(EXP, None, CTX),
            P(EXP, None, CTX),
            P(EXP, CTX, None),
            P(None, CTX),
            P(None, CTX),
            P(CTX, None),
        ),
        out_specs=P(AXES, None),
        check_vma=False,
    )
```

```python
import functools

import jax
import jax.numpy as jnp
from jax import lax
from jax.experimental import pallas as pl
from jax.experimental.pallas import tpu as pltpu
from jax.sharding import Mesh, PartitionSpec as P

H = 40
KVH = 8
HD = 128
F32 = jnp.float32
BF16 = jnp.bfloat16
AXES = ("x", "y", "zh", "zl", "core")
CTX = ("x", "y", "zh")
EXP = ("zl", "core")
LINE = ("zh", "zl", "core")


def shift(value, axis, by):
    n = lax.axis_size(axis)
    return lax.ppermute(value, axis, [(i, (i + by) % n) for i in range(n)])


def spread(value, axis):
    back = shift(value, axis, -1)
    ahead = shift(value, axis, 1)
    across = shift(value, axis, 2)
    return [value, ahead, across, back]


def ring(value, axis):
    ahead = shift(value, axis, 1)
    back = shift(value, axis, -1)
    half = value.shape[0] // 2
    across = [shift(ahead[:half], axis, 1), shift(back[half:], axis, -1)]
    return [value, ahead, back], across


def collect(terms, axis):
    ahead = shift(terms[1], axis, -1)
    back = shift(terms[3], axis, 1)
    across = shift(terms[2], axis, 2)
    return (
        terms[0].astype(F32) + ahead.astype(F32) + back.astype(F32) + across.astype(F32)
    ).astype(BF16)


def placed(parts, axis, dim):
    me = lax.axis_index(axis)
    n = len(parts)
    shape = list(parts[0].shape)
    size = shape[dim]
    shape[dim] = size * n
    out = jnp.zeros(shape, parts[0].dtype)
    for k, part in enumerate(parts):
        out = lax.dynamic_update_slice_in_dim(out, part, lax.rem(me - k + n, n) * size, dim)
    return out


def in_order(mine, other, index):
    return jnp.where(index == 0, jnp.stack([mine, other]), jnp.stack([other, mine]))


def mlp_kernel(pieces, depth_steps, *refs):
    slots, refs = refs[:pieces], refs[pieces:]
    column, gate, up, shared_gate, shared_up, down, shared_down = refs[:7]
    outs, (acc, score, hidden) = refs[7 : 7 + pieces], refs[7 + pieces :]
    step = pl.program_id(0)
    block = gate.shape[0]
    routed, shared = gate.shape[1], shared_gate.shape[1]
    count = slots[0].shape[0]

    @pl.when(step == 0)
    def _():
        acc[...] = jnp.zeros_like(acc)
        score[...] = jnp.zeros_like(score)

    @pl.when(step < depth_steps)
    def _():
        at = pl.multiple_of(step * block, block)
        x = jnp.concatenate([ref[:, pl.ds(at, block)] for ref in slots], axis=0)
        acc[:, :routed] += jnp.dot(x, gate[...], preferred_element_type=F32)
        acc[:, routed : 2 * routed] += jnp.dot(x, up[...], preferred_element_type=F32)
        acc[:, 2 * routed : 2 * routed + shared] += jnp.dot(
            x, shared_gate[...], preferred_element_type=F32
        )
        acc[:, 2 * routed + shared :] += jnp.dot(x, shared_up[...], preferred_element_type=F32)
        row = column[:, pl.ds(at, block)].astype(F32)
        sums = score[...]
        for k in range(block // 128):
            lanes = slice(k * 128, (k + 1) * 128)
            sums += x[:, lanes].astype(F32) * row[:, lanes]
        score[...] = sums

    @pl.when(step == depth_steps)
    def _():
        weight = jax.nn.sigmoid(jnp.sum(score[...], axis=1, keepdims=True))
        weight = weight.astype(BF16).astype(F32)
        a = acc[:, :routed] * weight
        b = acc[:, routed : 2 * routed] * weight
        hidden[:, :routed] = (a * jax.nn.sigmoid(a) * b).astype(BF16)
        a = acc[:, 2 * routed : 2 * routed + shared]
        b = acc[:, 2 * routed + shared :]
        hidden[:, routed:] = (a * jax.nn.sigmoid(a) * b).astype(BF16)

    @pl.when(step >= depth_steps)
    def _():
        result = jnp.dot(hidden[:, :routed], down[...], preferred_element_type=F32)
        result += jnp.dot(hidden[:, routed:], shared_down[...], preferred_element_type=F32)
        result = result.astype(BF16)
        for k, out in enumerate(outs):
            out[...] = result[k * count : (k + 1) * count]


def mlp(slots, column, gate, up, shared_gate, shared_up, down, shared_down):
    pieces, (count, features) = len(slots), slots[0].shape
    rows = pieces * count
    routed, shared = gate.shape[1], shared_gate.shape[1]
    steps, block = 4, features // 4
    whole = lambda shape: pl.BlockSpec(shape, lambda i: (0, 0))
    deep = lambda cols: pl.BlockSpec((block, cols), lambda i: (jnp.minimum(i, steps - 1), 0))
    wide = lambda rows: pl.BlockSpec((rows, block), lambda i: (0, jnp.maximum(i - steps, 0)))
    return pl.pallas_call(
        functools.partial(mlp_kernel, pieces, steps),
        grid=(2 * steps,),
        out_shape=[jax.ShapeDtypeStruct((count, features), BF16)] * pieces,
        in_specs=[whole((count, features))] * pieces
        + [whole((1, features)), deep(routed), deep(routed), deep(shared), deep(shared)]
        + [wide(routed), wide(shared)],
        out_specs=[wide(count)] * pieces,
        scratch_shapes=[
            pltpu.VMEM((rows, 2 * routed + 2 * shared), F32),
            pltpu.VMEM((rows, 128), F32),
            pltpu.VMEM((rows, routed + shared), BF16),
        ],
        compiler_params=pltpu.CompilerParams(vmem_limit_bytes=24 * 2**20),
        cost_estimate=pl.CostEstimate(
            flops=2 * rows * features * 3 * (routed + shared),
            bytes_accessed=2 * features * (3 * (routed + shared) + 2 * rows),
            transcendentals=rows * (routed + shared),
        ),
    )(*slots, column, gate, up, shared_gate, shared_up, down, shared_down)


def body(
    queries,
    keys,
    values,
    residual,
    span_order,
    out_weight,
    norm_gain,
    router,
    expert_ids,
    expert_gate,
    expert_up,
    expert_down,
    shared_gate,
    shared_up,
    shared_down,
):
    zh, core = lax.axis_index("zh"), lax.axis_index("core")
    rows = queries.shape[0]
    half = rows // 2
    group = H // KVH
    scale = HD ** (-0.5)
    features = residual.shape[1]

    pair = jnp.concatenate([keys, values], axis=1)
    pair_other = shift(pair, "zh", 1)
    both = jnp.concatenate([pair, pair_other], axis=0)
    sixteen = jnp.broadcast_to(both[None], (16,) + both.shape)
    everyone = lax.all_to_all(sixteen, ("x", "y"), split_axis=0, concat_axis=0)
    everyone = everyone.reshape(-1, 2 * HD)
    all_keys, all_values = everyone[:, :HD], everyone[:, HD:]
    spans = span_order.reshape(16, 2, 2)
    spans = jnp.where(zh == 0, spans, spans[:, ::-1])
    key_pos = (
        spans.reshape(-1)[:, None] * half + jnp.arange(half, dtype=jnp.int32)[None, :]
    ).reshape(-1)
    own = lax.dynamic_index_in_dim(span_order, lax.axis_index(CTX), 0, keepdims=False)
    own_pos = (own[:, None] * half + jnp.arange(half, dtype=jnp.int32)[None, :]).reshape(-1)

    turned = out_weight.T
    width = turned.shape[0] // 2
    w_mine = lax.dynamic_slice_in_dim(turned, core * width, width, 0)
    w_given = lax.dynamic_slice_in_dim(turned, (1 - core) * width, width, 0)
    w_pair = jnp.concatenate([w_mine, shift(w_given, "core", 1)], axis=1)
    w_pair = in_order(w_pair, shift(w_pair, "zh", 1), zh).reshape(1, 2 * width, -1)
    w_pair = placed(spread(w_pair, "y"), "y", 0).reshape(8 * width, -1)

    query_pos = jnp.tile(own_pos, group)
    grouped = queries.reshape(rows, group, HD).transpose(1, 0, 2).reshape(group * rows, HD)
    contract = (((1,), (1,)), ((), ()))
    visible = key_pos[None, :] <= query_pos[:, None]
    scores = lax.dot_general(grouped, all_keys, contract, preferred_element_type=F32) * scale
    top = jnp.max(jnp.where(visible, scores, -1e30), axis=1, keepdims=True)
    weights = jnp.where(visible, jnp.exp(scores - top), 0.0)
    total = jnp.sum(weights, axis=1, keepdims=True)
    mixed = jnp.dot(weights.astype(BF16), all_values, preferred_element_type=F32) / total
    attended = (
        mixed.astype(BF16).reshape(group, rows, HD).transpose(1, 0, 2).reshape(rows, group * HD)
    )

    a_pair = jnp.concatenate([attended, shift(attended, "core", 1)], axis=1)
    a_pair = placed(spread(a_pair, "x"), "x", 0)
    partial = lax.dot_general(a_pair, w_pair, contract, preferred_element_type=F32)
    partial = partial.astype(BF16).reshape(32, rows // 8, -1)
    pieces = lax.all_to_all(partial, ("x",) + EXP, split_axis=0, concat_axis=0)
    pieces = pieces.reshape(4, 4, 2, rows // 8, 8, width).astype(F32)
    projected = jnp.sum(pieces, axis=1).transpose(2, 0, 3, 1, 4).reshape(rows // 8, features)

    wide = (residual.astype(F32) + projected).astype(BF16).astype(F32)
    normed = (
        wide
        * lax.rsqrt(jnp.mean(wide * wide, axis=1, keepdims=True) + 1e-05)
        * norm_gain.astype(F32)
    ).astype(BF16)

    capacity = 2
    experts = router.shape[1]
    chosen = expert_ids[:, 0]
    onehot = (chosen[:, None] == jnp.arange(experts, dtype=jnp.int32)[None, :]).astype(jnp.int32)
    ranking = jnp.sum(jnp.cumsum(onehot, axis=0) * onehot, axis=1) - 1
    slot_index = chosen * capacity + ranking
    placing = slot_index[None, :] == jnp.arange(experts * capacity, dtype=jnp.int32)[:, None]
    send = jnp.dot(placing.astype(BF16), normed, preferred_element_type=F32).astype(BF16)
    send = send.reshape(1, experts, capacity, features)
    send = jnp.broadcast_to(send, (2, experts, capacity, features)).reshape(16, capacity, features)
    arrived = lax.all_to_all(send, LINE, split_axis=0, concat_axis=0)
    first, second = arrived[:, 0], arrived[:, 1]

    first = jnp.concatenate(spread(first, "x"), axis=0)
    second = jnp.concatenate(spread(second, "y"), axis=0)
    first, first_across = ring(first, "y")
    second, second_across = ring(second, "x")
    column = lax.dynamic_slice_in_dim(router, lax.axis_index(EXP), 1, 1).T
    held = (
        column,
        expert_gate[0],
        expert_up[0],
        shared_gate,
        shared_up,
        expert_down[0],
        shared_down,
    )
    outs = [mlp([a, b], *held) for a, b in zip(first, second)]
    across = mlp(first_across + second_across, *held)
    across = [jnp.concatenate(across[:2], axis=0), jnp.concatenate(across[2:], axis=0)]
    outs = [outs[0], outs[1], across, outs[2]]
    first = collect([o[0] for o in outs], "y")
    second = collect([o[1] for o in outs], "x")
    count = first.shape[0]
    quarter = count // 4
    first = collect([first[k * quarter : (k + 1) * quarter] for k in range(4)], "x")
    second = collect([second[k * quarter : (k + 1) * quarter] for k in range(4)], "y")
    back = lax.all_to_all(
        jnp.stack([first, second], axis=1), LINE, split_axis=0, concat_axis=0
    )
    back = jnp.sum(back.reshape(2, experts * capacity, features).astype(F32), axis=0)
    experts_out = jnp.dot(
        placing.astype(F32).T, back, precision=lax.Precision.HIGHEST, preferred_element_type=F32
    )
    return (wide + experts_out).astype(BF16)


def solution(mesh):
    fine = Mesh(mesh.devices.reshape(4, 4, 2, 4, 2), AXES)
    return jax.shard_map(
        body,
        mesh=fine,
        in_specs=(
            P(CTX, EXP),
            P(CTX, EXP),
            P(CTX, EXP),
            P(AXES, None),
            P(),
            P(EXP, CTX),
            P(),
            P(),
            P(AXES, None),
            P(EXP, None, CTX),
            P(EXP, None, CTX),
            P(EXP, CTX, None),
            P(None, CTX),
            P(None, CTX),
            P(CTX, None),
        ),
        out_specs=P(AXES, None),
        check_vma=False,
    )
```

```python
import functools

import jax
import jax.numpy as jnp
from jax import lax
from jax.experimental import pallas as pl
from jax.experimental.pallas import tpu as pltpu
from jax.sharding import Mesh, PartitionSpec as P

H = 40
KVH = 8
HD = 128
F32 = jnp.float32
BF16 = jnp.bfloat16
VMEM_LIMIT = 56 * 2**20
AXES = ("x", "y", "zh", "zl", "core")
CTX = ("x", "y", "zh")
EXP = ("zl", "core")
LINE = ("zh", "zl", "core")


def shift(value, axis, by):
    n = lax.axis_size(axis)
    return lax.ppermute(value, axis, [(i, (i + by) % n) for i in range(n)])


def spread(value, axis):
    back = shift(value, axis, -1)
    ahead = shift(value, axis, 1)
    across = shift(value, axis, 2)
    return [value, ahead, across, back]


def swap(value, axis, by):
    return lax.ppermute(value, axis, [(i, i ^ by) for i in range(4)])


def returned(ahead, across, back, axis):
    return [shift(ahead, axis, -1), shift(back, axis, 1), shift(across, axis, 2)]


def kept_kernel(*refs):
    mine, theirs, outs = refs[:8], refs[8:12], refs[12:]
    size = mine[0].shape[0]
    for k in range(8):
        other = theirs[k % 4][(k // 4) * size : (k // 4 + 1) * size, :]
        outs[k][...] = (mine[k][...].astype(F32) + other.astype(F32)).astype(BF16)


def total_kernel(*refs):
    kept, given, outs = refs[:4], refs[4:8], refs[8:]
    size = outs[0].shape[0]
    for k, out in enumerate(outs):
        at = slice((k % 2) * size, (k % 2 + 1) * size)
        out[...] = (kept[k // 2][at, :].astype(F32) + given[k // 2][at, :].astype(F32)).astype(BF16)


def elementwise(kernel, arrays, rows):
    columns = arrays[0].shape[1]
    block = columns // 5
    spec = lambda count: pl.BlockSpec((count, block), lambda i: (0, i))
    return pl.pallas_call(
        kernel,
        grid=(5,),
        out_shape=[jax.ShapeDtypeStruct((rows, columns), BF16)] * 8,
        in_specs=[spec(array.shape[0]) for array in arrays],
        out_specs=[spec(rows)] * 8,
        compiler_params=pltpu.CompilerParams(vmem_limit_bytes=12 * 2**20),
        cost_estimate=pl.CostEstimate(flops=1, bytes_accessed=1, transcendentals=0),
    )(*arrays)


def placed(parts, axis, dim):
    me = lax.axis_index(axis)
    n = len(parts)
    shape = list(parts[0].shape)
    size = shape[dim]
    shape[dim] = size * n
    out = jnp.zeros(shape, parts[0].dtype)
    for k, part in enumerate(parts):
        out = lax.dynamic_update_slice_in_dim(out, part, lax.rem(me - k + n, n) * size, dim)
    return out


def in_order(mine, other, index):
    return jnp.where(index == 0, jnp.stack([mine, other]), jnp.stack([other, mine]))


def mlp_kernel(pieces, results, steps, *refs):
    slots, refs = refs[:pieces], refs[pieces:]
    column, gate, up, shared_gate, shared_up, down, shared_down = refs[:7]
    outs, refs = refs[7 : 7 + results], refs[7 + results :]
    x, gate_v, up_v, shared_gate_v, shared_up_v, down_v, shared_down_v, acc, hidden, y = refs[:10]
    x_sem, in_sem, down_sem, out_sem = refs[10:]
    count, out_count = slots[0].shape[0], outs[0].shape[0]
    block = gate.shape[0] // steps
    routed, shared = gate.shape[1], shared_gate.shape[1]

    loads = [
        pltpu.make_async_copy(ref, x.at[pl.ds(k * count, count)], x_sem.at[k])
        for k, ref in enumerate(slots)
    ]
    deep = [
        [
            pltpu.make_async_copy(src.at[at], dst.at[at], in_sem.at[k, j])
            for j, (src, dst) in enumerate(
                (
                    (gate, gate_v),
                    (up, up_v),
                    (shared_gate, shared_gate_v),
                    (shared_up, shared_up_v),
                )
            )
        ]
        for k, at in enumerate(pl.ds(k * block, block) for k in range(steps))
    ]
    last = [
        pltpu.make_async_copy(down, down_v, down_sem.at[0]),
        pltpu.make_async_copy(shared_down, shared_down_v, down_sem.at[1]),
    ]
    for copy in loads + sum(deep, []) + last:
        copy.start()
    for copy in loads:
        copy.wait()
    score = jnp.zeros((x.shape[0], 128), F32)
    for k in range(steps):
        for copy in deep[k]:
            copy.wait()
        at = slice(k * block, (k + 1) * block)
        xk = x[:, at]
        base = 0
        for weight in (gate_v, up_v, shared_gate_v, shared_up_v):
            cols = slice(base, base + weight.shape[1])
            product = jnp.dot(xk, weight[at, :], preferred_element_type=F32)
            acc[:, cols] = product if k == 0 else acc[:, cols] + product
            base += weight.shape[1]
        row = column[:, at].astype(F32)
        for j in range(block // 128):
            lanes = slice(j * 128, (j + 1) * 128)
            score += xk[:, lanes].astype(F32) * row[:, lanes]
    weight = jax.nn.sigmoid(jnp.sum(score, axis=1, keepdims=True)).astype(BF16).astype(F32)
    a = acc[:, :routed] * weight
    b = acc[:, routed : 2 * routed] * weight
    hidden[:, :routed] = (a * jax.nn.sigmoid(a) * b).astype(BF16)
    a = acc[:, 2 * routed : 2 * routed + shared]
    b = acc[:, 2 * routed + shared :]
    hidden[:, routed:] = (a * jax.nn.sigmoid(a) * b).astype(BF16)
    for copy in last:
        copy.wait()
    stores = []
    for n in range(steps):
        at = slice(n * block, (n + 1) * block)
        result = jnp.dot(hidden[:, :routed], down_v[:, at], preferred_element_type=F32)
        result += jnp.dot(hidden[:, routed:], shared_down_v[:, at], preferred_element_type=F32)
        y[:, at] = result.astype(BF16)
        for k, out in enumerate(outs):
            stores.append(
                pltpu.make_async_copy(
                    y.at[pl.ds(k * out_count, out_count), pl.ds(n * block, block)],
                    out.at[:, pl.ds(n * block, block)],
                    out_sem.at[n, k],
                )
            )
            stores[-1].start()
    for copy in stores:
        copy.wait()


def mlp(slots, held, results, after=()):
    column, gate, up, shared_gate, shared_up, down, shared_down = held
    pieces, (count, features) = len(slots), slots[0].shape
    rows = pieces * count
    routed, shared = gate.shape[1], shared_gate.shape[1]
    steps = 4
    anywhere = pl.BlockSpec(memory_space=pl.ANY)
    kernel = functools.partial(mlp_kernel, pieces, results, steps)
    if after:
        plain = kernel
        kernel = lambda *refs: plain(*refs[len(after) :])
    return pl.pallas_call(
        kernel,
        out_shape=[jax.ShapeDtypeStruct((rows // results, features), BF16)] * results,
        in_specs=[anywhere] * (len(after) + pieces)
        + [pl.BlockSpec(memory_space=pltpu.VMEM)]
        + [anywhere] * 6,
        out_specs=[anywhere] * results,
        scratch_shapes=[
            pltpu.VMEM((rows, features), BF16),
            pltpu.VMEM(gate.shape, BF16),
            pltpu.VMEM(up.shape, BF16),
            pltpu.VMEM(shared_gate.shape, BF16),
            pltpu.VMEM(shared_up.shape, BF16),
            pltpu.VMEM(down.shape, BF16),
            pltpu.VMEM(shared_down.shape, BF16),
            pltpu.VMEM((rows, 2 * routed + 2 * shared), F32),
            pltpu.VMEM((rows, routed + shared), BF16),
            pltpu.VMEM((rows, features), BF16),
            pltpu.SemaphoreType.DMA((pieces,)),
            pltpu.SemaphoreType.DMA((steps, 4)),
            pltpu.SemaphoreType.DMA((2,)),
            pltpu.SemaphoreType.DMA((steps, results)),
        ],
        compiler_params=pltpu.CompilerParams(vmem_limit_bytes=VMEM_LIMIT),
        cost_estimate=pl.CostEstimate(flops=1, bytes_accessed=1, transcendentals=0),
    )(*after, *slots, *held)


def body(
    queries,
    keys,
    values,
    residual,
    span_order,
    out_weight,
    norm_gain,
    router,
    expert_ids,
    expert_gate,
    expert_up,
    expert_down,
    shared_gate,
    shared_up,
    shared_down,
):
    zh, core = lax.axis_index("zh"), lax.axis_index("core")
    rows = queries.shape[0]
    half = rows // 2
    group = H // KVH
    scale = HD ** (-0.5)
    features = residual.shape[1]

    pair = jnp.concatenate([keys, values], axis=1)
    pair_other = shift(pair, "zh", 1)
    both = jnp.concatenate([pair, pair_other], axis=0)
    sixteen = jnp.broadcast_to(both[None], (16,) + both.shape)
    everyone = lax.all_to_all(sixteen, ("x", "y"), split_axis=0, concat_axis=0)
    everyone = everyone.reshape(-1, 2 * HD)
    all_keys, all_values = everyone[:, :HD], everyone[:, HD:]
    spans = span_order.reshape(16, 2, 2)
    spans = jnp.where(zh == 0, spans, spans[:, ::-1])
    key_pos = (
        spans.reshape(-1)[:, None] * half + jnp.arange(half, dtype=jnp.int32)[None, :]
    ).reshape(-1)
    own = lax.dynamic_index_in_dim(span_order, lax.axis_index(CTX), 0, keepdims=False)
    own_pos = (own[:, None] * half + jnp.arange(half, dtype=jnp.int32)[None, :]).reshape(-1)

    turned = out_weight.T
    width = turned.shape[0] // 2
    w_both = in_order(turned, shift(turned, "zh", 1), zh)
    w_mine = lax.dynamic_slice_in_dim(w_both, core * width, width, 1)
    w_given = lax.dynamic_slice_in_dim(w_both, (1 - core) * width, width, 1)
    w_pair = jnp.concatenate([w_mine, shift(w_given, "core", 1)], axis=2)
    w_pair = w_pair.reshape(1, 2 * width, -1)
    w_parts = spread(w_pair, "y")

    query_pos = jnp.tile(own_pos, group)
    grouped = queries.reshape(rows, group, HD).transpose(1, 0, 2).reshape(group * rows, HD)
    contract = (((1,), (1,)), ((), ()))
    visible = key_pos[None, :] <= query_pos[:, None]
    scores = lax.dot_general(grouped, all_keys, contract, preferred_element_type=F32) * scale
    top = jnp.max(jnp.where(visible, scores, -1e30), axis=1, keepdims=True)
    weights = jnp.where(visible, jnp.exp(scores - top), 0.0)
    total = jnp.sum(weights, axis=1, keepdims=True)
    mixed = jnp.dot(weights.astype(BF16), all_values, preferred_element_type=F32) / total
    attended = (
        mixed.astype(BF16).reshape(group, rows, HD).transpose(1, 0, 2).reshape(rows, group * HD)
    )

    a_mine = placed(spread(attended[None], "x"), "x", 0)
    a_other = shift(a_mine, "core", 1)
    a_mine, a_other, *w_parts = lax.optimization_barrier((a_mine, a_other, *w_parts))
    w_pair = placed(w_parts, "y", 0).reshape(8 * width, -1)
    depth = attended.shape[1]
    partial = lax.dot_general(
        a_mine.reshape(4 * rows, depth), w_pair[:, :depth], contract, preferred_element_type=F32
    ) + lax.dot_general(
        a_other.reshape(4 * rows, depth), w_pair[:, depth:], contract, preferred_element_type=F32
    )
    partial = partial.astype(BF16).reshape(32, rows // 8, -1)
    pieces = lax.all_to_all(partial, ("x",) + EXP, split_axis=0, concat_axis=0)
    pieces = pieces.reshape(4, 4, 2, rows // 8, 8, width).astype(F32)
    projected = jnp.sum(pieces, axis=1).transpose(2, 0, 3, 1, 4).reshape(rows // 8, features)

    wide = (residual.astype(F32) + projected).astype(BF16).astype(F32)
    normed = (
        wide
        * lax.rsqrt(jnp.mean(wide * wide, axis=1, keepdims=True) + 1e-05)
        * norm_gain.astype(F32)
    ).astype(BF16)

    capacity = 2
    experts = router.shape[1]
    chosen = expert_ids[:, 0]
    onehot = (chosen[:, None] == jnp.arange(experts, dtype=jnp.int32)[None, :]).astype(jnp.int32)
    ranking = jnp.sum(jnp.cumsum(onehot, axis=0) * onehot, axis=1) - 1
    slot_index = chosen * capacity + ranking
    placing = slot_index[None, :] == jnp.arange(experts * capacity, dtype=jnp.int32)[:, None]
    send = jnp.dot(placing.astype(BF16), normed, preferred_element_type=F32).astype(BF16)
    send = send.reshape(1, experts, capacity, features)
    send = jnp.broadcast_to(send, (2, experts, capacity, features)).reshape(16, capacity, features)
    arrived = lax.all_to_all(send, LINE, split_axis=0, concat_axis=0)
    first, second = arrived[:, 0], arrived[:, 1]

    first, second = spread(first, "x"), spread(second, "y")
    start = [
        jnp.concatenate(part, axis=0) for part in (first[:2], first[2:], second[:2], second[2:])
    ]
    ways = (("y", 1, 3), ("y", 3, 1), ("x", 1, 3), ("x", 3, 1))
    near = [swap(value, axis, by) for value, (axis, by, _) in zip(start, ways)]
    far = [
        swap(jnp.concatenate(pair, axis=0), axis, by)
        for pair, (axis, _, by) in zip(zip(start, near), ways)
    ]
    column = lax.dynamic_slice_in_dim(router, lax.axis_index(EXP), 1, 1).T
    held = (
        column,
        expert_gate[0],
        expert_up[0],
        shared_gate,
        shared_up,
        expert_down[0],
        shared_down,
    )
    mine = mlp(start + near, held, 8)
    theirs = mlp(far, held, 4, after=mine)
    theirs = [swap(value, axis, by) for value, (axis, _, by) in zip(theirs, ways)]
    kept = elementwise(kept_kernel, [*mine, *theirs], start[0].shape[0])
    given = [swap(value, axis, by) for value, (axis, by, _) in zip(kept[4:], ways)]
    quarters = elementwise(total_kernel, [*kept[:4], *given], start[0].shape[0] // 2)
    first, second = quarters[:4], quarters[4:]
    first = [first[0]] + returned(*first[1:], "x")
    second = [second[0]] + returned(*second[1:], "y")
    first, second = (
        sum(term.astype(F32) for term in terms).astype(BF16) for terms in (first, second)
    )
    back = lax.all_to_all(
        jnp.stack([first, second], axis=1), LINE, split_axis=0, concat_axis=0
    )
    back = jnp.sum(back.reshape(2, experts * capacity, features).astype(F32), axis=0)
    experts_out = jnp.dot(
        placing.astype(F32).T, back, precision=lax.Precision.HIGHEST, preferred_element_type=F32
    )
    return (wide + experts_out).astype(BF16)


def solution(mesh):
    fine = Mesh(mesh.devices.reshape(4, 4, 2, 4, 2), AXES)
    return jax.shard_map(
        body,
        mesh=fine,
        in_specs=(
            P(CTX, EXP),
            P(CTX, EXP),
            P(CTX, EXP),
            P(AXES, None),
            P(),
            P(EXP, CTX),
            P(),
            P(),
            P(AXES, None),
            P(EXP, None, CTX),
            P(EXP, None, CTX),
            P(EXP, CTX, None),
            P(None, CTX),
            P(None, CTX),
            P(CTX, None),
        ),
        out_specs=P(AXES, None),
        check_vma=False,
    )
```

```python
import functools

import jax
import jax.numpy as jnp
from jax import lax
from jax.experimental import pallas as pl
from jax.experimental.pallas import tpu as pltpu
from jax.sharding import Mesh, PartitionSpec as P

H = 40
KVH = 8
HD = 128
F32 = jnp.float32
BF16 = jnp.bfloat16
VMEM_LIMIT = 40 * 2**20
AXES = ("x", "y", "zh", "zl", "core")
CTX = ("x", "y", "zh")
EXP = ("zl", "core")
LINE = ("zh", "zl", "core")


def shift(value, axis, by):
    n = lax.axis_size(axis)
    return lax.ppermute(value, axis, [(i, (i + by) % n) for i in range(n)])


def spread(value, axis):
    back = shift(value, axis, -1)
    ahead = shift(value, axis, 1)
    across = shift(value, axis, 2)
    return [value, ahead, across, back]


def swap(value, axis, by):
    return lax.ppermute(value, axis, [(i, i ^ by) for i in range(4)])


def returned(ahead, across, back, axis):
    return [shift(ahead, axis, -1), shift(back, axis, 1), shift(across, axis, 2)]


def kept_kernel(*refs):
    mine, theirs, outs = refs[:8], refs[8:12], refs[12:]
    size = mine[0].shape[0]
    for k in range(8):
        other = theirs[k % 4][(k // 4) * size : (k // 4 + 1) * size, :]
        outs[k][...] = (mine[k][...].astype(F32) + other.astype(F32)).astype(BF16)


def total_kernel(*refs):
    kept, given, outs = refs[:4], refs[4:8], refs[8:]
    size = outs[0].shape[0]
    for k, out in enumerate(outs):
        at = slice((k % 2) * size, (k % 2 + 1) * size)
        out[...] = (kept[k // 2][at, :].astype(F32) + given[k // 2][at, :].astype(F32)).astype(BF16)


def elementwise(kernel, arrays, rows):
    columns = arrays[0].shape[1]
    block = columns // 5
    spec = lambda count: pl.BlockSpec((count, block), lambda i: (0, i))
    return pl.pallas_call(
        kernel,
        grid=(5,),
        out_shape=[jax.ShapeDtypeStruct((rows, columns), BF16)] * 8,
        in_specs=[spec(array.shape[0]) for array in arrays],
        out_specs=[spec(rows)] * 8,
        compiler_params=pltpu.CompilerParams(vmem_limit_bytes=12 * 2**20),
        cost_estimate=pl.CostEstimate(flops=1, bytes_accessed=1, transcendentals=0),
    )(*arrays)


def placed(parts, axis, dim):
    me = lax.axis_index(axis)
    n = len(parts)
    shape = list(parts[0].shape)
    size = shape[dim]
    shape[dim] = size * n
    out = jnp.zeros(shape, parts[0].dtype)
    for k, part in enumerate(parts):
        out = lax.dynamic_update_slice_in_dim(out, part, lax.rem(me - k + n, n) * size, dim)
    return out


def in_place(pairs, one, two, index):
    size = pairs[0].shape[0] // 2
    out = jnp.zeros((4 * size,) + pairs[0].shape[1:], pairs[0].dtype)
    for pair, first in zip(pairs, (index, index ^ two)):
        for part, at in ((pair[:size], first), (pair[size:], first ^ one)):
            out = lax.dynamic_update_slice_in_dim(out, part, at * size, 0)
    return out


def in_order(mine, other, index):
    return jnp.where(index == 0, jnp.stack([mine, other]), jnp.stack([other, mine]))


def mlp_kernel(pieces, results, steps, held, *refs):
    slots, refs = refs[:pieces], refs[pieces:]
    column, gate, up, shared_gate, shared_up, down, shared_down = refs[:7]
    outs, refs = refs[7 : 7 + results], refs[7 + results :]
    if held:
        gate_v, up_v, shared_gate_v, shared_up_v = gate, up, shared_gate, shared_up
        down_v, shared_down_v = down, shared_down
    else:
        gate_v, up_v, shared_gate_v, shared_up_v, down_v, shared_down_v = refs[:6]
        refs = refs[6:]
    x, acc, hidden, y = refs[:4]
    refs = refs[4:]
    x_sem, in_sem, down_sem, out_sem = refs
    count, out_count = slots[0].shape[0], outs[0].shape[0]
    block = gate.shape[0] // steps
    routed, shared = gate.shape[1], shared_gate.shape[1]

    loads = [
        pltpu.make_async_copy(ref, x.at[pl.ds(k * count, count)], x_sem.at[k])
        for k, ref in enumerate(slots)
    ]
    deep = [] if held else [
        [
            pltpu.make_async_copy(src.at[at], dst.at[at], in_sem.at[k, j])
            for j, (src, dst) in enumerate(
                (
                    (gate, gate_v),
                    (up, up_v),
                    (shared_gate, shared_gate_v),
                    (shared_up, shared_up_v),
                )
            )
        ]
        for k, at in enumerate(pl.ds(k * block, block) for k in range(steps))
    ]
    last = [] if held else [
        pltpu.make_async_copy(down, down_v, down_sem.at[0]),
        pltpu.make_async_copy(shared_down, shared_down_v, down_sem.at[1]),
    ]
    for copy in loads if held else loads + sum(deep, []) + last:
        copy.start()
    for copy in loads:
        copy.wait()
    score = jnp.zeros((x.shape[0], 128), F32)
    for k in range(steps):
        for copy in () if held else deep[k]:
            copy.wait()
        at = slice(k * block, (k + 1) * block)
        xk = x[:, at]
        base = 0
        for weight in (gate_v, up_v, shared_gate_v, shared_up_v):
            cols = slice(base, base + weight.shape[1])
            product = jnp.dot(xk, weight[at, :], preferred_element_type=F32)
            acc[:, cols] = product if k == 0 else acc[:, cols] + product
            base += weight.shape[1]
        row = column[:, at].astype(F32)
        for j in range(block // 128):
            lanes = slice(j * 128, (j + 1) * 128)
            score += xk[:, lanes].astype(F32) * row[:, lanes]
    weight = jax.nn.sigmoid(jnp.sum(score, axis=1, keepdims=True)).astype(BF16).astype(F32)
    a = acc[:, :routed] * weight
    b = acc[:, routed : 2 * routed] * weight
    hidden[:, :routed] = (a * jax.nn.sigmoid(a) * b).astype(BF16)
    a = acc[:, 2 * routed : 2 * routed + shared]
    b = acc[:, 2 * routed + shared :]
    hidden[:, routed:] = (a * jax.nn.sigmoid(a) * b).astype(BF16)
    for copy in () if held else last:
        copy.wait()
    stores = []
    for n in range(steps):
        at = slice(n * block, (n + 1) * block)
        result = jnp.dot(hidden[:, :routed], down_v[:, at], preferred_element_type=F32)
        result += jnp.dot(hidden[:, routed:], shared_down_v[:, at], preferred_element_type=F32)
        y[:, at] = result.astype(BF16)
        for k, out in enumerate(outs):
            stores.append(
                pltpu.make_async_copy(
                    y.at[pl.ds(k * out_count, out_count), pl.ds(n * block, block)],
                    out.at[:, pl.ds(n * block, block)],
                    out_sem.at[n, k],
                )
            )
            stores[-1].start()
    for copy in stores:
        copy.wait()


def mlp(slots, weights, results, held, after=()):
    column, gate, up, shared_gate, shared_up, down, shared_down = weights
    pieces, (count, features) = len(slots), slots[0].shape
    rows = pieces * count
    routed, shared = gate.shape[1], shared_gate.shape[1]
    steps = 4
    anywhere = pl.BlockSpec(memory_space=pl.ANY)
    inside = pl.BlockSpec(memory_space=pltpu.VMEM)
    kernel = functools.partial(mlp_kernel, pieces, results, steps, held)
    if after:
        plain = kernel
        kernel = lambda *refs: plain(*refs[len(after) :])
    if held:
        weights = [column] + [
            pltpu.with_memory_space_constraint(weight, pltpu.VMEM) for weight in weights[1:]
        ]
    kept = () if held else weights[1:]
    outs = pl.pallas_call(
        kernel,
        out_shape=[jax.ShapeDtypeStruct((rows // results, features), BF16)] * results
        + [pltpu.VMEM(weight.shape, BF16) for weight in kept],
        in_specs=[anywhere] * (len(after) + pieces)
        + [inside]
        + [inside if held else anywhere] * 6,
        out_specs=[anywhere] * results + [inside] * len(kept),
        scratch_shapes=[
            pltpu.VMEM((rows, features), BF16),
            pltpu.VMEM((rows, 2 * routed + 2 * shared), F32),
            pltpu.VMEM((rows, routed + shared), BF16),
            pltpu.VMEM((rows, features), BF16),
            pltpu.SemaphoreType.DMA((pieces,)),
            pltpu.SemaphoreType.DMA((steps, 4)),
            pltpu.SemaphoreType.DMA((2,)),
            pltpu.SemaphoreType.DMA((steps, results)),
        ],
        compiler_params=pltpu.CompilerParams(vmem_limit_bytes=VMEM_LIMIT),
        cost_estimate=pl.CostEstimate(flops=1, bytes_accessed=1, transcendentals=0),
    )(*after, *slots, *weights)
    return outs[:results], [column, *outs[results:]]


def body(
    queries,
    keys,
    values,
    residual,
    span_order,
    out_weight,
    norm_gain,
    router,
    expert_ids,
    expert_gate,
    expert_up,
    expert_down,
    shared_gate,
    shared_up,
    shared_down,
):
    zh, core = lax.axis_index("zh"), lax.axis_index("core")
    rows = queries.shape[0]
    half = rows // 2
    group = H // KVH
    scale = HD ** (-0.5)
    features = residual.shape[1]

    pair = jnp.concatenate([keys, values], axis=1)
    pair_other = shift(pair, "zh", 1)
    both = jnp.concatenate([pair, pair_other], axis=0)
    sixteen = jnp.broadcast_to(both[None], (16,) + both.shape)
    everyone = lax.all_to_all(sixteen, ("x", "y"), split_axis=0, concat_axis=0)
    everyone = everyone.reshape(-1, 2 * HD)
    all_keys, all_values = everyone[:, :HD], everyone[:, HD:]
    spans = span_order.reshape(16, 2, 2)
    spans = jnp.where(zh == 0, spans, spans[:, ::-1])
    key_pos = (
        spans.reshape(-1)[:, None] * half + jnp.arange(half, dtype=jnp.int32)[None, :]
    ).reshape(-1)
    own = lax.dynamic_index_in_dim(span_order, lax.axis_index(CTX), 0, keepdims=False)
    own_pos = (own[:, None] * half + jnp.arange(half, dtype=jnp.int32)[None, :]).reshape(-1)

    turned = out_weight.T
    width = turned.shape[0] // 2
    w_both = in_order(turned, shift(turned, "zh", 1), zh)
    w_mine = lax.dynamic_slice_in_dim(w_both, core * width, width, 1)
    w_given = lax.dynamic_slice_in_dim(w_both, (1 - core) * width, width, 1)
    w_halves = []
    for value, one, two in ((w_mine, 1, 3), (shift(w_given, "core", 1), 3, 1)):
        value = value.reshape(1, 2 * width, -1)
        pair = jnp.concatenate([value, swap(value, "y", one)], axis=0)
        w_halves += [pair, swap(pair, "y", two)]

    query_pos = jnp.tile(own_pos, group)
    grouped = queries.reshape(rows, group, HD).transpose(1, 0, 2).reshape(group * rows, HD)
    contract = (((1,), (1,)), ((), ()))
    visible = key_pos[None, :] <= query_pos[:, None]
    scores = lax.dot_general(grouped, all_keys, contract, preferred_element_type=F32) * scale
    top = jnp.max(jnp.where(visible, scores, -1e30), axis=1, keepdims=True)
    weights = jnp.where(visible, jnp.exp(scores - top), 0.0)
    total = jnp.sum(weights, axis=1, keepdims=True)
    mixed = jnp.dot(weights.astype(BF16), all_values, preferred_element_type=F32) / total
    attended = (
        mixed.astype(BF16).reshape(group, rows, HD).transpose(1, 0, 2).reshape(rows, group * HD)
    )

    a_mine = placed(spread(attended[None], "x"), "x", 0)
    a_other = shift(a_mine, "core", 1)
    a_mine, a_other, *w_halves = lax.optimization_barrier((a_mine, a_other, *w_halves))
    depth = attended.shape[1]
    y = lax.axis_index("y")
    partial = sum(
        lax.dot_general(
            a.reshape(4 * rows, depth),
            in_place(pairs, one, two, y).reshape(8 * width, depth),
            contract,
            preferred_element_type=F32,
        )
        for a, pairs, one, two in (
            (a_mine, w_halves[:2], 1, 3),
            (a_other, w_halves[2:], 3, 1),
        )
    )
    partial = partial.astype(BF16).reshape(32, rows // 8, -1)
    pieces = lax.all_to_all(partial, ("x",) + EXP, split_axis=0, concat_axis=0)
    pieces = pieces.reshape(4, 4, 2, rows // 8, 8, width).astype(F32)
    projected = jnp.sum(pieces, axis=1).transpose(2, 0, 3, 1, 4).reshape(rows // 8, features)

    wide = (residual.astype(F32) + projected).astype(BF16).astype(F32)
    normed = (
        wide
        * lax.rsqrt(jnp.mean(wide * wide, axis=1, keepdims=True) + 1e-05)
        * norm_gain.astype(F32)
    ).astype(BF16)

    capacity = 2
    experts = router.shape[1]
    chosen = expert_ids[:, 0]
    onehot = (chosen[:, None] == jnp.arange(experts, dtype=jnp.int32)[None, :]).astype(jnp.int32)
    ranking = jnp.sum(jnp.cumsum(onehot, axis=0) * onehot, axis=1) - 1
    slot_index = chosen * capacity + ranking
    placing = slot_index[None, :] == jnp.arange(experts * capacity, dtype=jnp.int32)[:, None]
    send = jnp.dot(placing.astype(BF16), normed, preferred_element_type=F32).astype(BF16)
    send = send.reshape(1, experts, capacity, features)
    send = jnp.broadcast_to(send, (2, experts, capacity, features)).reshape(16, capacity, features)
    arrived = lax.all_to_all(send, LINE, split_axis=0, concat_axis=0)
    first, second = arrived[:, 0], arrived[:, 1]

    first, second = spread(first, "x"), spread(second, "y")
    start = [
        jnp.concatenate(part, axis=0) for part in (first[:2], first[2:], second[:2], second[2:])
    ]
    ways = (("y", 1, 3), ("y", 3, 1), ("x", 1, 3), ("x", 3, 1))
    near = [swap(value, axis, by) for value, (axis, by, _) in zip(start, ways)]
    far = [
        swap(jnp.concatenate(pair, axis=0), axis, by)
        for pair, (axis, _, by) in zip(zip(start, near), ways)
    ]
    column = lax.dynamic_slice_in_dim(router, lax.axis_index(EXP), 1, 1).T
    held = (
        column,
        expert_gate[0],
        expert_up[0],
        shared_gate,
        shared_up,
        expert_down[0],
        shared_down,
    )
    mine, held = mlp(start + near, held, 8, False)
    theirs, _ = mlp(far, held, 4, True, after=mine)
    theirs = [swap(value, axis, by) for value, (axis, _, by) in zip(theirs, ways)]
    kept = elementwise(kept_kernel, [*mine, *theirs], start[0].shape[0])
    given = [swap(value, axis, by) for value, (axis, by, _) in zip(kept[4:], ways)]
    quarters = elementwise(total_kernel, [*kept[:4], *given], start[0].shape[0] // 2)
    first, second = quarters[:4], quarters[4:]
    first = [first[0]] + returned(*first[1:], "x")
    second = [second[0]] + returned(*second[1:], "y")
    first, second = (
        sum(term.astype(F32) for term in terms).astype(BF16) for terms in (first, second)
    )
    back = lax.all_to_all(
        jnp.stack([first, second], axis=1), LINE, split_axis=0, concat_axis=0
    )
    back = jnp.sum(back.reshape(2, experts * capacity, features).astype(F32), axis=0)
    experts_out = jnp.dot(
        placing.astype(F32).T, back, precision=lax.Precision.HIGHEST, preferred_element_type=F32
    )
    return (wide + experts_out).astype(BF16)


def solution(mesh):
    fine = Mesh(mesh.devices.reshape(4, 4, 2, 4, 2), AXES)
    return jax.shard_map(
        body,
        mesh=fine,
        in_specs=(
            P(CTX, EXP),
            P(CTX, EXP),
            P(CTX, EXP),
            P(AXES, None),
            P(),
            P(EXP, CTX),
            P(),
            P(),
            P(AXES, None),
            P(EXP, None, CTX),
            P(EXP, None, CTX),
            P(EXP, CTX, None),
            P(None, CTX),
            P(None, CTX),
            P(CTX, None),
        ),
        out_specs=P(AXES, None),
        check_vma=False,
    )
```

```python
import functools

import jax
import jax.numpy as jnp
from jax import lax
from jax.experimental import pallas as pl
from jax.experimental.pallas import tpu as pltpu
from jax.sharding import Mesh, PartitionSpec as P

H = 40
KVH = 8
HD = 128
F32 = jnp.float32
BF16 = jnp.bfloat16
VMEM_LIMIT = 40 * 2**20
AXES = ("x", "y", "zh", "zl", "core")
CTX = ("x", "y", "zh")
EXP = ("zl", "core")
LINE = ("zh", "zl", "core")


def shift(value, axis, by):
    n = lax.axis_size(axis)
    return lax.ppermute(value, axis, [(i, (i + by) % n) for i in range(n)])


def spread(value, axis):
    back = shift(value, axis, -1)
    ahead = shift(value, axis, 1)
    across = shift(value, axis, 2)
    return [value, ahead, across, back]


def swap(value, axis, by):
    return lax.ppermute(value, axis, [(i, i ^ by) for i in range(4)])


def returned(ahead, across, back, axis):
    return [shift(ahead, axis, -1), shift(back, axis, 1), shift(across, axis, 2)]


def kept_kernel(*refs):
    mine, theirs, outs = refs[:8], refs[8:12], refs[12:]
    size = mine[0].shape[0]
    for k in range(8):
        other = theirs[k % 4][(k // 4) * size : (k // 4 + 1) * size, :]
        outs[k][...] = (mine[k][...].astype(F32) + other.astype(F32)).astype(BF16)


def total_kernel(*refs):
    kept, given, outs = refs[:4], refs[4:8], refs[8:]
    size = outs[0].shape[0]
    for k, out in enumerate(outs):
        at = slice((k % 2) * size, (k % 2 + 1) * size)
        out[...] = (kept[k // 2][at, :].astype(F32) + given[k // 2][at, :].astype(F32)).astype(BF16)


def elementwise(kernel, arrays, rows):
    columns = arrays[0].shape[1]
    block = columns // 5
    spec = lambda count: pl.BlockSpec((count, block), lambda i: (0, i))
    return pl.pallas_call(
        kernel,
        grid=(5,),
        out_shape=[jax.ShapeDtypeStruct((rows, columns), BF16)] * 8,
        in_specs=[spec(array.shape[0]) for array in arrays],
        out_specs=[spec(rows)] * 8,
        compiler_params=pltpu.CompilerParams(vmem_limit_bytes=12 * 2**20),
        cost_estimate=pl.CostEstimate(flops=1, bytes_accessed=1, transcendentals=0),
    )(*arrays)


def placed(parts, axis, dim):
    me = lax.axis_index(axis)
    n = len(parts)
    shape = list(parts[0].shape)
    size = shape[dim]
    shape[dim] = size * n
    out = jnp.zeros(shape, parts[0].dtype)
    for k, part in enumerate(parts):
        out = lax.dynamic_update_slice_in_dim(out, part, lax.rem(me - k + n, n) * size, dim)
    return out


def in_place(pairs, one, two, index):
    size = pairs[0].shape[0] // 2
    out = jnp.zeros((4 * size,) + pairs[0].shape[1:], pairs[0].dtype)
    for pair, first in zip(pairs, (index, index ^ two)):
        for part, at in ((pair[:size], first), (pair[size:], first ^ one)):
            out = lax.dynamic_update_slice_in_dim(out, part, at * size, 0)
    return out


def in_order(mine, other, index):
    return jnp.where(index == 0, jnp.stack([mine, other]), jnp.stack([other, mine]))


def mlp_kernel(pieces, results, steps, held, *refs):
    slots, refs = refs[:pieces], refs[pieces:]
    column, gate, up, shared_gate, shared_up, down, shared_down = refs[:7]
    outs, refs = refs[7 : 7 + results], refs[7 + results :]
    if held:
        gate_v, up_v, shared_gate_v, shared_up_v = gate, up, shared_gate, shared_up
        down_v, shared_down_v = down, shared_down
    else:
        gate_v, up_v, shared_gate_v, shared_up_v, down_v, shared_down_v = refs[:6]
        refs = refs[6:]
    x, acc, hidden, y = refs[:4]
    refs = refs[4:]
    x_sem, in_sem, down_sem, out_sem = refs
    count, out_count = slots[0].shape[0], outs[0].shape[0]
    block = gate.shape[0] // steps
    routed, shared = gate.shape[1], shared_gate.shape[1]

    loads = [
        [
            pltpu.make_async_copy(
                ref.at[:, pl.ds(n * block, block)],
                x.at[pl.ds(k * count, count), pl.ds(n * block, block)],
                x_sem.at[n, k],
            )
            for k, ref in enumerate(slots)
        ]
        for n in range(steps)
    ]
    deep = [] if held else [
        [
            pltpu.make_async_copy(src.at[at], dst.at[at], in_sem.at[k, j])
            for j, (src, dst) in enumerate(
                (
                    (gate, gate_v),
                    (up, up_v),
                    (shared_gate, shared_gate_v),
                    (shared_up, shared_up_v),
                )
            )
        ]
        for k, at in enumerate(pl.ds(k * block, block) for k in range(steps))
    ]
    last = [] if held else [
        pltpu.make_async_copy(down, down_v, down_sem.at[0]),
        pltpu.make_async_copy(shared_down, shared_down_v, down_sem.at[1]),
    ]
    for copy in sum(loads + deep, []) + last:
        copy.start()
    score = jnp.zeros((x.shape[0], 128), F32)
    for k in range(steps):
        for copy in loads[k] if held else loads[k] + deep[k]:
            copy.wait()
        at = slice(k * block, (k + 1) * block)
        xk = x[:, at]
        base = 0
        for weight in (gate_v, up_v, shared_gate_v, shared_up_v):
            cols = slice(base, base + weight.shape[1])
            product = jnp.dot(xk, weight[at, :], preferred_element_type=F32)
            acc[:, cols] = product if k == 0 else acc[:, cols] + product
            base += weight.shape[1]
        row = column[:, at].astype(F32)
        for j in range(block // 128):
            lanes = slice(j * 128, (j + 1) * 128)
            score += xk[:, lanes].astype(F32) * row[:, lanes]
    weight = jax.nn.sigmoid(jnp.sum(score, axis=1, keepdims=True)).astype(BF16).astype(F32)
    a = acc[:, :routed] * weight
    b = acc[:, routed : 2 * routed] * weight
    hidden[:, :routed] = (a * jax.nn.sigmoid(a) * b).astype(BF16)
    a = acc[:, 2 * routed : 2 * routed + shared]
    b = acc[:, 2 * routed + shared :]
    hidden[:, routed:] = (a * jax.nn.sigmoid(a) * b).astype(BF16)
    for copy in last:
        copy.wait()
    stores = []
    for n in range(steps):
        at = slice(n * block, (n + 1) * block)
        result = jnp.dot(hidden[:, :routed], down_v[:, at], preferred_element_type=F32)
        result += jnp.dot(hidden[:, routed:], shared_down_v[:, at], preferred_element_type=F32)
        y[:, at] = result.astype(BF16)
        for k, out in enumerate(outs):
            stores.append(
                pltpu.make_async_copy(
                    y.at[pl.ds(k * out_count, out_count), pl.ds(n * block, block)],
                    out.at[:, pl.ds(n * block, block)],
                    out_sem.at[n, k],
                )
            )
            stores[-1].start()
    for copy in stores:
        copy.wait()


def mlp(slots, weights, results, held, after=()):
    column, gate, up, shared_gate, shared_up, down, shared_down = weights
    pieces, (count, features) = len(slots), slots[0].shape
    rows = pieces * count
    routed, shared = gate.shape[1], shared_gate.shape[1]
    steps = 4
    anywhere = pl.BlockSpec(memory_space=pl.ANY)
    inside = pl.BlockSpec(memory_space=pltpu.VMEM)
    kernel = functools.partial(mlp_kernel, pieces, results, steps, held)
    if after:
        plain = kernel
        kernel = lambda *refs: plain(*refs[len(after) :])
    if held:
        weights = [column] + [
            pltpu.with_memory_space_constraint(weight, pltpu.VMEM) for weight in weights[1:]
        ]
    kept = () if held else weights[1:]
    outs = pl.pallas_call(
        kernel,
        out_shape=[jax.ShapeDtypeStruct((rows // results, features), BF16)] * results
        + [pltpu.VMEM(weight.shape, BF16) for weight in kept],
        in_specs=[anywhere] * (len(after) + pieces)
        + [inside]
        + [inside if held else anywhere] * 6,
        out_specs=[anywhere] * results + [inside] * len(kept),
        scratch_shapes=[
            pltpu.VMEM((rows, features), BF16),
            pltpu.VMEM((rows, 2 * routed + 2 * shared), F32),
            pltpu.VMEM((rows, routed + shared), BF16),
            pltpu.VMEM((rows, features), BF16),
            pltpu.SemaphoreType.DMA((steps, pieces)),
            pltpu.SemaphoreType.DMA((steps, 4)),
            pltpu.SemaphoreType.DMA((2,)),
            pltpu.SemaphoreType.DMA((steps, results)),
        ],
        compiler_params=pltpu.CompilerParams(vmem_limit_bytes=VMEM_LIMIT),
        cost_estimate=pl.CostEstimate(flops=1, bytes_accessed=1, transcendentals=0),
    )(*after, *slots, *weights)
    return outs[:results], [column, *outs[results:]]


def body(
    queries,
    keys,
    values,
    residual,
    span_order,
    out_weight,
    norm_gain,
    router,
    expert_ids,
    expert_gate,
    expert_up,
    expert_down,
    shared_gate,
    shared_up,
    shared_down,
):
    zh, core = lax.axis_index("zh"), lax.axis_index("core")
    rows = queries.shape[0]
    half = rows // 2
    group = H // KVH
    scale = HD ** (-0.5)
    features = residual.shape[1]

    pair = jnp.concatenate([keys, values], axis=1)
    pair_other = shift(pair, "zh", 1)
    both = jnp.concatenate([pair, pair_other], axis=0)
    sixteen = jnp.broadcast_to(both[None], (16,) + both.shape)
    everyone = lax.all_to_all(sixteen, ("x", "y"), split_axis=0, concat_axis=0)
    everyone = everyone.reshape(-1, 2 * HD)
    all_keys, all_values = everyone[:, :HD], everyone[:, HD:]
    spans = span_order.reshape(16, 2, 2)
    spans = jnp.where(zh == 0, spans, spans[:, ::-1])
    key_pos = (
        spans.reshape(-1)[:, None] * half + jnp.arange(half, dtype=jnp.int32)[None, :]
    ).reshape(-1)
    own = lax.dynamic_index_in_dim(span_order, lax.axis_index(CTX), 0, keepdims=False)
    own_pos = (own[:, None] * half + jnp.arange(half, dtype=jnp.int32)[None, :]).reshape(-1)

    turned = out_weight.T
    width = turned.shape[0] // 2
    w_both = in_order(turned, shift(turned, "zh", 1), zh)
    w_mine = lax.dynamic_slice_in_dim(w_both, core * width, width, 1)
    w_given = lax.dynamic_slice_in_dim(w_both, (1 - core) * width, width, 1)
    w_halves = []
    for value, one, two in ((w_mine, 1, 3), (shift(w_given, "core", 1), 3, 1)):
        value = value.reshape(1, 2 * width, -1)
        pair = jnp.concatenate([value, swap(value, "y", one)], axis=0)
        w_halves += [pair, swap(pair, "y", two)]

    query_pos = jnp.tile(own_pos, group)
    grouped = queries.reshape(rows, group, HD).transpose(1, 0, 2).reshape(group * rows, HD)
    contract = (((1,), (1,)), ((), ()))
    visible = key_pos[None, :] <= query_pos[:, None]
    scores = lax.dot_general(grouped, all_keys, contract, preferred_element_type=F32) * scale
    top = jnp.max(jnp.where(visible, scores, -1e30), axis=1, keepdims=True)
    weights = jnp.where(visible, jnp.exp(scores - top), 0.0)
    total = jnp.sum(weights, axis=1, keepdims=True)
    mixed = jnp.dot(weights.astype(BF16), all_values, preferred_element_type=F32) / total
    attended = (
        mixed.astype(BF16).reshape(group, rows, HD).transpose(1, 0, 2).reshape(rows, group * HD)
    )

    a_mine = placed(spread(attended[None], "x"), "x", 0)
    a_other = shift(a_mine, "core", 1)
    a_mine, a_other, *w_halves = lax.optimization_barrier((a_mine, a_other, *w_halves))
    depth = attended.shape[1]
    y = lax.axis_index("y")
    partial = sum(
        lax.dot_general(
            a.reshape(4 * rows, depth),
            in_place(pairs, one, two, y).reshape(8 * width, depth),
            contract,
            preferred_element_type=F32,
        )
        for a, pairs, one, two in (
            (a_mine, w_halves[:2], 1, 3),
            (a_other, w_halves[2:], 3, 1),
        )
    )
    partial = partial.astype(BF16).reshape(32, rows // 8, -1)
    pieces = lax.all_to_all(partial, ("x",) + EXP, split_axis=0, concat_axis=0)
    pieces = pieces.reshape(4, 4, 2, rows // 8, 8, width).astype(F32)
    projected = jnp.sum(pieces, axis=1).transpose(2, 0, 3, 1, 4).reshape(rows // 8, features)

    wide = (residual.astype(F32) + projected).astype(BF16).astype(F32)
    normed = (
        wide
        * lax.rsqrt(jnp.mean(wide * wide, axis=1, keepdims=True) + 1e-05)
        * norm_gain.astype(F32)
    ).astype(BF16)

    capacity = 2
    experts = router.shape[1]
    chosen = expert_ids[:, 0]
    onehot = (chosen[:, None] == jnp.arange(experts, dtype=jnp.int32)[None, :]).astype(jnp.int32)
    ranking = jnp.sum(jnp.cumsum(onehot, axis=0) * onehot, axis=1) - 1
    slot_index = chosen * capacity + ranking
    placing = slot_index[None, :] == jnp.arange(experts * capacity, dtype=jnp.int32)[:, None]
    send = jnp.dot(placing.astype(BF16), normed, preferred_element_type=F32).astype(BF16)
    send = send.reshape(1, experts, capacity, features)
    send = jnp.broadcast_to(send, (2, experts, capacity, features)).reshape(16, capacity, features)
    arrived = lax.all_to_all(send, LINE, split_axis=0, concat_axis=0)
    first, second = arrived[:, 0], arrived[:, 1]

    first, second = spread(first, "x"), spread(second, "y")
    start = [
        jnp.concatenate(part, axis=0) for part in (first[:2], first[2:], second[:2], second[2:])
    ]
    ways = (("y", 1, 3), ("y", 3, 1), ("x", 1, 3), ("x", 3, 1))
    near = [swap(value, axis, by) for value, (axis, by, _) in zip(start, ways)]
    far = [
        swap(jnp.concatenate(pair, axis=0), axis, by)
        for pair, (axis, _, by) in zip(zip(start, near), ways)
    ]
    column = lax.dynamic_slice_in_dim(router, lax.axis_index(EXP), 1, 1).T
    held = (
        column,
        expert_gate[0],
        expert_up[0],
        shared_gate,
        shared_up,
        expert_down[0],
        shared_down,
    )
    mine, held = mlp(start + near, held, 8, False)
    theirs, _ = mlp(far, held, 4, True, after=mine)
    theirs = [swap(value, axis, by) for value, (axis, _, by) in zip(theirs, ways)]
    kept = elementwise(kept_kernel, [*mine, *theirs], start[0].shape[0])
    given = [swap(value, axis, by) for value, (axis, by, _) in zip(kept[4:], ways)]
    quarters = elementwise(total_kernel, [*kept[:4], *given], start[0].shape[0] // 2)
    first, second = quarters[:4], quarters[4:]
    first = [first[0]] + returned(*first[1:], "x")
    second = [second[0]] + returned(*second[1:], "y")
    first, second = (
        sum(term.astype(F32) for term in terms).astype(BF16) for terms in (first, second)
    )
    back = lax.all_to_all(
        jnp.stack([first, second], axis=1), LINE, split_axis=0, concat_axis=0
    )
    back = jnp.sum(back.reshape(2, experts * capacity, features).astype(F32), axis=0)
    experts_out = jnp.dot(
        placing.astype(F32).T, back, precision=lax.Precision.HIGHEST, preferred_element_type=F32
    )
    return (wide + experts_out).astype(BF16)


def solution(mesh):
    fine = Mesh(mesh.devices.reshape(4, 4, 2, 4, 2), AXES)
    return jax.shard_map(
        body,
        mesh=fine,
        in_specs=(
            P(CTX, EXP),
            P(CTX, EXP),
            P(CTX, EXP),
            P(AXES, None),
            P(),
            P(EXP, CTX),
            P(),
            P(),
            P(AXES, None),
            P(EXP, None, CTX),
            P(EXP, None, CTX),
            P(EXP, CTX, None),
            P(None, CTX),
            P(None, CTX),
            P(CTX, None),
        ),
        out_specs=P(AXES, None),
        check_vma=False,
    )
```
